32 devices in a mesh: groups: 2 (over y), blk: 4 (over z), panel: 4 (over x, core).
Axes of the slice: x: 2, y: 2, z: 4, core: 2. Of those that a mesh axis runs over, the one named last changes fastest.
Arguments:
- test_features: bfloat16 [2048, 8192], P(('groups', 'blk'), 'panel'), parts along dimension 0, may hold values from -6 to 6
- train_features: bfloat16 [2048, 8192], P(('groups', 'blk'), 'panel'), parts along dimension 0, may hold values from -0.0625 to 0.0625
- kernel_inverse: bfloat16 [8192, 8192], P('panel', 'blk'), as said below
Outputs:
- scores: float32 [2048, 1024], P(('groups', 'panel'), 'blk'), parts along dimension 0
The draws below stay inside these ranges and needn't reach their ends.
There are 2 independent parts, one for each index of `groups`. The reference program is written for one: setup_inputs(seed, part) draws one part's arguments, and reference() takes and returns one part's arrays. A program takes and returns all parts, laid end to end along the dimension named above; an argument that names none is the same for every part. Nothing has to cross between parts.
Inputs may be any that keep to these rules, and one draw needn't show every extreme that they name: kernel_inverse is symmetric.
All inputs are finite; a program needn't handle non-finite values.
Results may differ from the reference program's by a relative error of at most 0.0029.
Values may be sent and summed in bfloat16 or wider, within the bound.
A program may use at most 128 MiB of HBM per device.

```python
import math
import jax
import jax.numpy as jnp

K = 8192
NT = 1024
NR = 1024


def draw_kernel_inverse(key, part):
    key = jax.random.fold_in(key, 7)
    first, second = jax.random.split(key)
    base = jax.random.normal(first, (K, K), jnp.float32)
    diag_terms = jnp.exp(jax.random.uniform(second, (K,), jnp.float32, math.log(0.25), math.log(2.0)))
    symmetric = (base + base.T) * (0.70710678 / math.sqrt(K))
    eye_mask = jnp.arange(K)[:, None] == jnp.arange(K)[None, :]
    total = symmetric + jnp.where(eye_mask, diag_terms[None, :], 0.0)
    return total.astype(jnp.bfloat16)


def steps_of(key, dims, cuts, least, top_value):
    loudness, own = 1.0, jax.random.fold_in(key, 6)
    for dim, shards_of in cuts:
        steps = jnp.exp(jax.random.uniform(jax.random.fold_in(own, dim), (shards_of,), jnp.float32, least / len(cuts), top_value / len(cuts)))
        loudness = loudness * jnp.repeat(steps, dims[dim] // shards_of).reshape([-1 if axis == dim else 1 for axis in range(len(dims))])
    return loudness


def normal_values(stream_key, shape, width, limit, shards=(), held_as=jnp.bfloat16):
    result = jax.random.normal(stream_key, shape, jnp.float32) * width
    if len(shards) > 0:
        result = steps_of(stream_key, shape, shards, -0.22, 0.18) * result
    return jnp.clip(result, min=-limit, max=limit).astype(held_as)


def setup_inputs(seed: int = 0, part: int = 0) -> dict:
    keys = jax.random.split(jax.random.key(seed), 4)
    part_splits = jax.random.split(jax.random.fold_in(keys[3], part), 4)
    test_features = normal_values(part_splits[0], (NT, K), 1.0, 6.0, ((0, 4), (1, 4)))
    train_features = normal_values(part_splits[1], (NR, K), K ** -0.5, 0.0625, ((0, 4), (1, 4)))
    kernel_inverse = draw_kernel_inverse(jax.random.fold_in(keys[3], 71), part)
    return dict(test_features=test_features, train_features=train_features, kernel_inverse=kernel_inverse)


def reference(test_features, train_features, kernel_inverse):
    preconditioned = jnp.dot(test_features, kernel_inverse, preferred_element_type=jnp.float32).astype(jnp.bfloat16)
    return jnp.dot(preconditioned, train_features.T, preferred_element_type=jnp.float32)
```

```python
import functools

import jax
import jax.numpy as jnp
from jax import lax
from jax.experimental import pallas as pl
from jax.experimental.pallas import tpu as pltpu
from jax.sharding import PartitionSpec as P

MESH = pl.DeviceIdType.MESH
VMEM_BYTES = 56 * 1024 * 1024


def local(test_features, train_features, kernel_inverse):
    all_rows = lax.all_gather(test_features, "blk", axis=0, tiled=True)
    slab_terms = jnp.dot(all_rows, kernel_inverse, preferred_element_type=jnp.float32)
    reduced = lax.psum_scatter(slab_terms, "panel", scatter_dimension=0, tiled=True).astype(
        jnp.bfloat16
    )
    preconditioned = lax.all_to_all(
        lax.all_to_all(reduced, "blk", split_axis=0, concat_axis=1, tiled=True),
        "panel",
        split_axis=1,
        concat_axis=0,
        tiled=True,
    )
    partial_scores = lax.dot_general(
        lax.all_gather(preconditioned, "blk", axis=0, tiled=True),
        train_features,
        (((1,), (1,)), ((), ())),
        preferred_element_type=jnp.float32,
    )
    blocks = lax.axis_size("blk")
    panels = lax.axis_size("panel")
    total_rows = partial_scores.shape[0]
    width = partial_scores.shape[1]
    grouped = partial_scores.reshape(blocks, panels, total_rows // (blocks * panels), width)
    partial_scores = jnp.transpose(grouped, (1, 0, 2, 3)).reshape(total_rows, width)
    return lax.psum_scatter(partial_scores, "panel", scatter_dimension=0, tiled=True)


def kernel(
    n, tile, t_ref, r_ref, k_ref, out_ref,
    tbuf, rbuf, stage, kbuf, sbuf, crecv, xrecv, zrecv,
    lsem, tsend, trecv, rsend, rrecv, gsend, grecv, csend, crsem, xsend, xrsem, zsend, zrsem,
):
    rows, depth = t_ref.shape
    half = rows // 2
    g = lax.axis_index("groups")
    b = lax.axis_index("blk")
    p = lax.axis_index("panel")
    sib = p + 1 - 2 * lax.rem(p, 2)
    peer = lax.rem(p + 2, 4)

    def at(blk, panel):
        return (g, blk, panel)

    def remote(src, dst, send, recv, blk, panel):
        return pltpu.make_async_remote_copy(
            src_ref=src, dst_ref=dst, send_sem=send, recv_sem=recv,
            device_id=at(blk, panel), device_id_type=MESH,
        )

    barrier = pltpu.get_barrier_semaphore()
    for k in range(1, n):
        pl.semaphore_signal(barrier, inc=1, device_id=at(lax.rem(b + k, n), p), device_id_type=MESH)
    pl.semaphore_signal(barrier, inc=1, device_id=at(b, sib), device_id_type=MESH)
    pl.semaphore_signal(barrier, inc=1, device_id=at(b, peer), device_id_type=MESH)

    load_k = pltpu.make_async_copy(k_ref, kbuf, lsem.at[0])
    load_t = pltpu.make_async_copy(t_ref, tbuf.at[b], lsem.at[1])
    load_r = pltpu.make_async_copy(r_ref, rbuf.at[b], lsem.at[2])
    pl.semaphore_wait(barrier, n + 1)

    diag = b == p
    across = b == peer
    entry = lax.rem(b, 2) == lax.rem(p, 2)
    top = pl.ds(0, half)
    low = pl.ds(half, half)

    own_top = remote(r_ref.at[top], rbuf.at[b, top], rsend.at[0], rrecv.at[b, 0], p, p)
    own_low = remote(r_ref.at[low], stage, rsend.at[1], grecv, b, peer)
    own_peer = remote(r_ref, rbuf.at[b], rsend.at[0], rrecv.at[b, 0], b, peer)
    own_sib = remote(r_ref, rbuf.at[b], rsend.at[1], rrecv.at[b, 0], b, sib)

    @pl.when(jnp.logical_not(diag))
    def _():
        own_low.start()
        own_top.start()

    @pl.when(diag)
    def _():
        own_peer.start()
        own_sib.start()

    def t_copy(src, c, way, blk):
        return remote(src, tbuf.at[c], tsend.at[way, c], trecv.at[c], blk, p)

    @pl.when(b > 0)
    def _():
        t_copy(t_ref, b, 0, b - 1).start()

    @pl.when(b < n - 1)
    def _():
        t_copy(t_ref, b, 1, b + 1).start()

    load_t.start()
    load_k.start()

    @pl.when(diag)
    def _():
        load_r.start()

    go_on = remote(stage, rbuf.at[b, low], gsend, rrecv.at[b, 1], peer, p)

    @pl.when(jnp.logical_not(across))
    def _():
        remote(stage, stage, gsend, grecv, b, peer).wait_recv()
        go_on.start()

    def r_part(j, which):
        start = pl.multiple_of(which * half, half)
        return rbuf.at[j, pl.ds(start, half)]

    def r_move(j, which, way, panel):
        return remote(
            r_part(j, which), r_part(j, which), rsend.at[2 + j * 4 + way],
            rrecv.at[j, which], b, panel,
        )

    mine = jnp.where(diag, 0, 1)

    @pl.when(entry)
    def _():
        @pl.when(across)
        def _():
            remote(rbuf.at[b], rbuf.at[b], rsend.at[0], rrecv.at[b, 0], b, peer).wait_recv()
            remote(rbuf.at[b], rbuf.at[b], rsend.at[2 + 4 * n], rrecv.at[b, 0], b, sib).start()

        for k in (1, n - 1, 2):
            j = lax.rem(b + k, n)
            r_move(j, mine, 0, peer).wait_recv()
            r_move(j, mine, 0, peer).start()
            r_move(j, mine, 1, sib).start()

    def arrive(c, blk, way, more):
        t_copy(tbuf.at[c], c, way, blk).wait_recv()

        @pl.when(more)
        def _():
            t_copy(tbuf.at[c], c, way, blk).start()

    def arrivals(k):
        @pl.when(b - k >= 0)
        def _():
            arrive(b - k, lax.rem(b + 1, n), 1, b < n - 1)

        @pl.when(b + k < n)
        def _():
            arrive(b + k, lax.rem(b + n - 1, n), 0, b > 0)

    def compute(c):
        sbuf[c] = jnp.zeros_like(sbuf[c])

        def step(t, carry):
            cols = pl.ds(pl.multiple_of(t * tile, tile), tile)
            part = jnp.dot(tbuf[c], kbuf[:, cols], preferred_element_type=jnp.float32)
            hi = part.astype(jnp.bfloat16)
            lo = (part - hi.astype(jnp.float32)).astype(jnp.bfloat16)
            for j in range(n):
                right = rbuf[j, :, cols]
                dims = (((1,), (1,)), ((), ()))
                sbuf[c, j] += lax.dot_general(
                    hi, right, dims, preferred_element_type=jnp.float32
                ) + lax.dot_general(lo, right, dims, preferred_element_type=jnp.float32)
            return carry

        lax.fori_loop(0, depth // tile, step, 0)

        other = lax.rem(c, 2) != lax.rem(p, 2)
        copy = remote(sbuf.at[c], crecv.at[c], csend.at[c], crsem.at[c], b, sib)

        @pl.when(other)
        def _():
            copy.start()

        @pl.when(jnp.logical_not(other))
        def _():
            copy.wait_recv()
            sbuf[c] += crecv[c]

            @pl.when(c != p)
            def _():
                remote(sbuf.at[c], xrecv, xsend, xrsem, b, peer).start()

    def z_copy(k):
        to = lax.rem(b + k, n)
        return remote(sbuf.at[p, to], zrecv.at[b], zsend.at[k - 1], zrsem.at[b], to, p)

    def spread(c):
        @pl.when(c == p)
        def _():
            remote(sbuf.at[c], xrecv, xsend, xrsem, b, peer).wait_recv()
            sbuf[c] += xrecv[...]
            for k in range(1, n):
                z_copy(k).start()

    def at_step(k, f):
        @pl.when(b - k >= 0)
        def _():
            f(b - k)

        @pl.when(b + k < n)
        def _():
            f(b + k)

    arrivals(1)

    @pl.when(entry)
    def _():
        for k in (1, n - 1, 2):
            j = lax.rem(b + k, n)
            r_move(j, 1 - mine, 0, peer).wait_recv()
            r_move(j, 1 - mine, 2, sib).start()

    @pl.when(jnp.logical_not(entry))
    def _():
        remote(rbuf.at[b], rbuf.at[b], rsend.at[0], rrecv.at[b, 0], b, sib).wait_recv()
        for k in (1, n - 1, 2):
            j = lax.rem(b + k, n)
            r_move(j, 0, 0, sib).wait_recv()
            r_move(j, 1, 0, sib).wait_recv()

    load_t.wait()
    load_k.wait()

    @pl.when(diag)
    def _():
        load_r.wait()

    compute(b)
    for k in range(1, n):
        if k > 1:
            arrivals(k)
        at_step(k, compute)
        if k == 1:
            spread(b)
        else:
            at_step(k - 1, spread)
    at_step(n - 1, spread)

    total = sbuf[p, b]
    for k in range(1, n):
        j = lax.rem(b + k, n)
        remote(zrecv.at[j], zrecv.at[j], zsend.at[k - 1], zrsem.at[j], j, p).wait_recv()
        total = total + zrecv[j]
    out_ref[...] = total

    @pl.when(jnp.logical_not(diag))
    def _():
        own_top.wait_send()
        own_low.wait_send()

    @pl.when(diag)
    def _():
        own_peer.wait_send()
        own_sib.wait_send()

    @pl.when(b > 0)
    def _():
        t_copy(t_ref, b, 0, b - 1).wait_send()

    @pl.when(b < n - 1)
    def _():
        t_copy(t_ref, b, 1, b + 1).wait_send()

    @pl.when(jnp.logical_not(across))
    def _():
        go_on.wait_send()

    @pl.when(entry)
    def _():
        @pl.when(across)
        def _():
            remote(rbuf.at[b], rbuf.at[b], rsend.at[2 + 4 * n], rrecv.at[b, 0], b, sib).wait_send()

        for k in range(1, n):
            j = lax.rem(b + k, n)
            r_move(j, mine, 0, peer).wait_send()
            r_move(j, mine, 1, sib).wait_send()
            r_move(j, 1 - mine, 2, sib).wait_send()

    for k in range(1, n):
        @pl.when(jnp.logical_and(b - k >= 0, b < n - 1))
        def _():
            t_copy(tbuf.at[b - k], b - k, 1, b + 1).wait_send()

        @pl.when(jnp.logical_and(b + k < n, b > 0))
        def _():
            t_copy(tbuf.at[b + k], b + k, 0, b - 1).wait_send()

    for c in range(n):
        @pl.when(c % 2 != lax.rem(p, 2))
        def _():
            remote(sbuf.at[c], crecv.at[c], csend.at[c], crsem.at[c], b, sib).wait_send()

    remote(sbuf.at[peer], xrecv, xsend, xrsem, b, peer).wait_send()
    for k in range(1, n):
        z_copy(k).wait_send()


def fused(n, test_features, train_features, kernel_inverse):
    rows, depth = test_features.shape
    bf16, f32 = jnp.bfloat16, jnp.float32
    dma = pltpu.SemaphoreType.DMA
    return pl.pallas_call(
        functools.partial(kernel, n, min(512, depth)),
        out_shape=jax.ShapeDtypeStruct((rows, rows), f32),
        in_specs=[pl.BlockSpec(memory_space=pl.ANY)] * 3,
        out_specs=pl.BlockSpec(memory_space=pltpu.VMEM),
        scratch_shapes=[
            pltpu.VMEM((n, rows, depth), bf16),
            pltpu.VMEM((n, rows, depth), bf16),
            pltpu.VMEM((rows // 2, depth), bf16),
            pltpu.VMEM((depth, depth), bf16),
            pltpu.VMEM((n, n, rows, rows), f32),
            pltpu.VMEM((n, n, rows, rows), f32),
            pltpu.VMEM((n, rows, rows), f32),
            pltpu.VMEM((n, rows, rows), f32),
            dma((3,)),
            dma((2, n)),
            dma((n,)),
            dma((3 + 4 * n,)),
            dma((n, 2)),
            dma,
            dma,
            dma((n,)),
            dma((n,)),
            dma,
            dma,
            dma((n,)),
            dma((n,)),
        ],
        compiler_params=pltpu.CompilerParams(
            collective_id=0, has_side_effects=True, vmem_limit_bytes=VMEM_BYTES
        ),
        cost_estimate=pl.CostEstimate(
            flops=2 * n * rows * depth * (depth + 2 * n * rows),
            bytes_accessed=2 * depth * (depth + 2 * rows) + 4 * rows * rows,
            transcendentals=0,
        ),
    )(test_features, train_features, kernel_inverse)


def held_bytes(n, rows, depth):
    return 4 * n * rows * depth + 2 * depth * depth + 8 * n * rows * n * rows


def solution(mesh):
    in_specs = (P(("groups", "blk"), "panel"), P(("groups", "blk"), "panel"), P("panel", "blk"))
    out_specs = P(("groups", "panel"), "blk")
    blocks, panels = mesh.shape["blk"], mesh.shape["panel"]

    def run(test_features, train_features, kernel_inverse):
        rows, depth = test_features.shape
        same = train_features.shape == (rows, depth) and kernel_inverse.shape == (depth, depth)
        if blocks == 4 and panels == 4 and same and held_bytes(blocks, rows, depth) < VMEM_BYTES * 3 // 4:
            return fused(blocks, test_features, train_features, kernel_inverse)
        return local(test_features, train_features, kernel_inverse)

    return jax.shard_map(run, mesh=mesh, in_specs=in_specs, out_specs=out_specs, check_vma=False)
```

```python
import functools

import jax
import jax.numpy as jnp
from jax import lax
from jax.experimental import pallas as pl
from jax.experimental.pallas import tpu as pltpu
from jax.sharding import PartitionSpec as P

MESH = pl.DeviceIdType.MESH
VMEM_BYTES = 56 * 1024 * 1024


def local(test_features, train_features, kernel_inverse):
    all_rows = lax.all_gather(test_features, "blk", axis=0, tiled=True)
    slab_terms = jnp.dot(all_rows, kernel_inverse, preferred_element_type=jnp.float32)
    reduced = lax.psum_scatter(slab_terms, "panel", scatter_dimension=0, tiled=True).astype(
        jnp.bfloat16
    )
    preconditioned = lax.all_to_all(
        lax.all_to_all(reduced, "blk", split_axis=0, concat_axis=1, tiled=True),
        "panel",
        split_axis=1,
        concat_axis=0,
        tiled=True,
    )
    partial_scores = lax.dot_general(
        lax.all_gather(preconditioned, "blk", axis=0, tiled=True),
        train_features,
        (((1,), (1,)), ((), ())),
        preferred_element_type=jnp.float32,
    )
    blocks = lax.axis_size("blk")
    panels = lax.axis_size("panel")
    total_rows = partial_scores.shape[0]
    width = partial_scores.shape[1]
    grouped = partial_scores.reshape(blocks, panels, total_rows // (blocks * panels), width)
    partial_scores = jnp.transpose(grouped, (1, 0, 2, 3)).reshape(total_rows, width)
    return lax.psum_scatter(partial_scores, "panel", scatter_dimension=0, tiled=True)


def kernel(
    n, tile, t_ref, r_ref, k_ref, out_ref,
    tbuf, rbuf, tmore, rmore, stage, kbuf, sbuf, crecv, xrecv, zrecv, fbuf, home,
    lsem, tsend, trecv, msend, mrecv, rsend, rrecv, qsend, qrecv, gsend, grecv,
    csend, crsem, xsend, xrsem, zsend, zrsem, fsend, frsem,
):
    rows, depth = t_ref.shape
    half, quarter = rows // 2, rows // 4
    g = lax.axis_index("groups")
    b = lax.axis_index("blk")
    p = lax.axis_index("panel")
    core, chip = lax.rem(p, 2), p // 2
    sib = p + 1 - 2 * core
    peer = lax.rem(p + 2, 4)
    far = peer + 1 - 2 * core

    def at(blk, panel):
        return (g, blk, panel)

    def remote(src, dst, send, recv, blk, panel):
        return pltpu.make_async_remote_copy(
            src_ref=src, dst_ref=dst, send_sem=send, recv_sem=recv,
            device_id=at(blk, panel), device_id_type=MESH,
        )

    def on(condition, f, *args):
        @pl.when(condition)
        def _():
            f(*args)

    def both(*conditions):
        return functools.reduce(jnp.logical_and, conditions)

    barrier = pltpu.get_barrier_semaphore()
    partners = [at(lax.rem(b + k, n), p) for k in range(1, n)]
    partners += [at(b, sib), at(b, peer), at(b, far)]
    for partner in partners:
        pl.semaphore_signal(barrier, inc=1, device_id=partner, device_id_type=MESH)
    load_k = pltpu.make_async_copy(k_ref, kbuf, lsem.at[0])
    load_t = pltpu.make_async_copy(t_ref, tbuf.at[b], lsem.at[1])
    load_r = pltpu.make_async_copy(r_ref, rbuf.at[b], lsem.at[2])
    load_m = pltpu.make_async_copy(r_ref, rmore.at[b], lsem.at[2])
    pl.semaphore_wait(barrier, n + 2)

    diag = b == p
    outer = jnp.logical_or(p == 0, p == 3)
    helper_blk = jnp.where(p == 0, 1, 2)
    helper = both(outer, b == helper_blk)
    giver = both(jnp.logical_not(outer), diag)
    first = jnp.where(p == 1, 1, 0)
    last = jnp.where(p == 2, n - 2, n - 1)
    active = both(b >= first, b <= last)
    go_left, go_right = both(b - 1 >= first, b > 0), both(b + 1 <= last, b < n - 1)
    left, right = lax.rem(b + n - 1, n), lax.rem(b + 1, n)
    entry_panel = 3 * lax.rem(b, 2)
    entry = p == entry_panel
    entry_peer = peer == entry_panel
    staged = both(outer, b != peer)

    r_stage = remote(r_ref, stage, rsend.at[0], grecv, b, peer)
    r_more = remote(r_ref, rmore.at[b], rsend.at[0], qrecv.at[b], helper_blk, p)
    r_end = remote(r_ref, rbuf.at[b], rsend.at[0], rrecv.at[b], p, p)
    r_peer = remote(r_ref, rbuf.at[b], rsend.at[1], rrecv.at[b], b, peer)
    r_sib = remote(r_ref, rbuf.at[b], rsend.at[2], rrecv.at[b], b, sib)
    stages = both(jnp.logical_not(outer), jnp.logical_not(diag))
    mores = both(outer, b != helper_blk)
    on(stages, r_stage.start)
    on(mores, r_more.start)
    on(helper, r_end.start)
    on(diag, r_peer.start)
    on(diag, r_sib.start)

    def t_copy(src, c, way):
        return remote(src, tbuf.at[c], tsend.at[way, c], trecv.at[c], right if way else left, p)

    def t_more(src, c):
        return remote(src, tmore.at[c], msend.at[c], mrecv.at[c], b, sib)

    on(go_left, t_copy(t_ref, b, 0).start)
    on(go_right, t_copy(t_ref, b, 1).start)
    load_t.start()
    load_k.start()
    on(diag, load_r.start)
    on(helper, load_m.start)
    on(giver, t_more(t_ref, b).start)

    r_on = remote(stage, rbuf.at[b], gsend, rrecv.at[b], peer, p)

    @pl.when(staged)
    def _():
        r_stage.wait_recv()
        r_on.start()

    def r_move(j, way):
        to = peer if way == 0 else sib
        return remote(rbuf.at[j], rbuf.at[j], rsend.at[3 + 2 * j + way], rrecv.at[j], b, to)

    def r_pass(j):
        return remote(rmore.at[j], rbuf.at[j], qsend.at[j], rrecv.at[j], p, p)

    def arrivals(k):
        def arrive(c, way, more):
            t_copy(tbuf.at[c], c, way).wait_recv()
            on(more, t_copy(tbuf.at[c], c, way).start)
            on(giver, t_more(tbuf.at[c], c).start)

        on(both(b - k >= 0, b <= last), arrive, b - k, 1, go_right)
        on(both(b + k < n, b >= first), arrive, b + k, 0, go_left)

    def more_arrives(j):
        remote(rmore.at[j], rmore.at[j], qsend.at[j], qrecv.at[j], b, p).wait_recv()
        on(j != p, r_pass(j).start)

    def entry_arrives(j):
        r_move(j, 0).wait_recv()
        r_move(j, 0).start()
        r_move(j, 1).start()

    def peer_arrives(j):
        r_move(j, 1).wait_recv()
        r_move(j, 1).start()

    near = [lax.rem(b + k, n) for k in (1, n - 1, 2)]

    def compute(c):
        sbuf[c] = jnp.zeros_like(sbuf[c])
        dims = (((1,), (1,)), ((), ()))

        def add(part, train, cols):
            hi = part.astype(jnp.bfloat16)
            lo = (part - hi.astype(jnp.float32)).astype(jnp.bfloat16)
            for j in range(n):
                block = train[j, :, cols]
                sbuf[c, j] += lax.dot_general(
                    hi, block, dims, preferred_element_type=jnp.float32
                ) + lax.dot_general(lo, block, dims, preferred_element_type=jnp.float32)

        def step(t, carry):
            cols = pl.ds(pl.multiple_of(t * tile, tile), tile)
            add(jnp.dot(tbuf[c], kbuf[:, cols], preferred_element_type=jnp.float32), rbuf, cols)
            return carry

        def step_more(t, carry):
            cols = pl.ds(pl.multiple_of(t * tile, tile), tile)
            part = lax.dot_general(
                tmore[c], kbuf[cols, :], dims, preferred_element_type=jnp.float32
            )
            add(part, rmore, cols)
            return carry

        @pl.when(active)
        def _():
            lax.fori_loop(0, depth // tile, step, 0)

        @pl.when(helper)
        def _():
            t_more(tmore.at[c], c).wait_recv()
            lax.fori_loop(0, depth // tile, step_more, 0)

        core_copy(c).start()

    def span(start, size):
        return pl.ds(pl.multiple_of(start, quarter), size)

    own_half = span(core * half, half)
    sib_half = span((1 - core) * half, half)
    own_part = span(core * half + chip * quarter, quarter)
    peer_part = span(core * half + (1 - chip) * quarter, quarter)

    def core_copy(c):
        return remote(sbuf.at[c, :, sib_half], crecv.at[c], csend.at[c], crsem.at[c], b, sib)

    def chip_copy(c):
        return remote(sbuf.at[c, :, peer_part], xrecv.at[c], xsend.at[c], xrsem.at[c], b, peer)

    def plane_copy(c, k):
        to = lax.rem(b + k, n)
        return remote(
            sbuf.at[c, to, own_part], zrecv.at[b, c], zsend.at[c, k - 1], zrsem.at[b, c], to, p
        )

    def join_cores(c):
        core_copy(c).wait_recv()
        sbuf[c, :, own_half] += crecv[c]
        chip_copy(c).start()

    def join_chips(c):
        chip_copy(c).wait_recv()
        sbuf[c, :, own_part] += xrecv[c]
        for k in range(1, n):
            plane_copy(c, k).start()

    def at_step(k, f):
        if k == 0:
            f(b)
        else:
            on(b - k >= 0, f, b - k)
            on(b + k < n, f, b + k)

    arrivals(1)

    @pl.when(helper)
    def _():
        for j in near:
            more_arrives(j)

    @pl.when(entry)
    def _():
        for j in near:
            entry_arrives(j)
        on(jnp.logical_not(diag), peer_arrives, b)

    arrivals(2)

    @pl.when(entry_peer)
    def _():
        on(jnp.logical_not(diag), peer_arrives, b)
        for j in near:
            peer_arrives(j)

    @pl.when(jnp.logical_not(jnp.logical_or(entry, entry_peer)))
    def _():
        for j in range(n):
            r_move(j, 1).wait_recv()

    load_t.wait()
    load_k.wait()
    on(diag, load_r.wait)
    on(helper, load_m.wait)

    for k in range(n):
        if k > 2:
            arrivals(k)
        at_step(k, compute)
        at_step(k, join_cores)
        if k > 0:
            at_step(k - 1, join_chips)
    at_step(n - 1, join_chips)

    def home_copy(c):
        return remote(fbuf.at[c], home.at[p], fsend.at[c], frsem.at[p], b, c)

    for c in range(n):
        total = sbuf[c, b, own_part]
        for k in range(1, n):
            j = lax.rem(b + k, n)
            remote(zrecv.at[j, c], zrecv.at[j, c], zsend.at[c, 0], zrsem.at[j, c], j, p).wait_recv()
            total = total + zrecv[j, c]
        fbuf[c] = total
        on(p != c, home_copy(c).start)
    out_ref[own_part, :] = fbuf[p]
    for q in range(n):
        @pl.when(p != q)
        def _():
            remote(home.at[q], home.at[q], fsend.at[q], frsem.at[q], b, q).wait_recv()
            start = (q % 2) * half + (q // 2) * quarter
            out_ref[start:start + quarter, :] = home[q]

    on(stages, r_stage.wait_send)
    on(mores, r_more.wait_send)
    on(helper, r_end.wait_send)
    on(diag, r_peer.wait_send)
    on(diag, r_sib.wait_send)
    on(go_left, t_copy(t_ref, b, 0).wait_send)
    on(go_right, t_copy(t_ref, b, 1).wait_send)
    on(giver, t_more(t_ref, b).wait_send)
    on(staged, r_on.wait_send)

    @pl.when(helper)
    def _():
        for j in near:
            on(j != p, r_pass(j).wait_send)

    @pl.when(entry)
    def _():
        for j in near:
            r_move(j, 0).wait_send()
            r_move(j, 1).wait_send()
        on(jnp.logical_not(diag), r_move(b, 1).wait_send)

    @pl.when(entry_peer)
    def _():
        for j in near:
            r_move(j, 1).wait_send()
        on(jnp.logical_not(diag), r_move(b, 1).wait_send)

    def t_left_all(c, way, more):
        on(more, t_copy(tbuf.at[c], c, way).wait_send)
        on(giver, t_more(tbuf.at[c], c).wait_send)

    for k in range(1, n):
        on(both(b - k >= 0, b <= last), t_left_all, b - k, 1, go_right)
        on(both(b + k < n, b >= first), t_left_all, b + k, 0, go_left)
    for c in range(n):
        core_copy(c).wait_send()
        chip_copy(c).wait_send()
        for k in range(1, n):
            plane_copy(c, k).wait_send()
        on(p != c, home_copy(c).wait_send)


def fused(n, test_features, train_features, kernel_inverse):
    rows, depth = test_features.shape
    bf16, f32 = jnp.bfloat16, jnp.float32
    dma = pltpu.SemaphoreType.DMA
    return pl.pallas_call(
        functools.partial(kernel, n, min(512, depth)),
        out_shape=jax.ShapeDtypeStruct((rows, rows), f32),
        in_specs=[pl.BlockSpec(memory_space=pl.ANY)] * 3,
        out_specs=pl.BlockSpec(memory_space=pltpu.VMEM),
        scratch_shapes=[
            pltpu.VMEM((n, rows, depth), bf16),
            pltpu.VMEM((n, rows, depth), bf16),
            pltpu.VMEM((n, rows, depth), bf16),
            pltpu.VMEM((n, rows, depth), bf16),
            pltpu.VMEM((rows, depth), bf16),
            pltpu.VMEM((depth, depth), bf16),
            pltpu.VMEM((n, n, rows, rows), f32),
            pltpu.VMEM((n, n, rows // 2, rows), f32),
            pltpu.VMEM((n, n, rows // 4, rows), f32),
            pltpu.VMEM((n, n, rows // 4, rows), f32),
            pltpu.VMEM((n, rows // 4, rows), f32),
            pltpu.VMEM((n, rows // 4, rows), f32),
            dma((3,)),
            dma((2, n)),
            dma((n,)),
            dma((n,)),
            dma((n,)),
            dma((3 + 2 * n,)),
            dma((n,)),
            dma((n,)),
            dma((n,)),
            dma,
            dma,
            dma((n,)),
            dma((n,)),
            dma((n,)),
            dma((n,)),
            dma((n, n - 1)),
            dma((n, n)),
            dma((n,)),
            dma((n,)),
        ],
        compiler_params=pltpu.CompilerParams(
            collective_id=0, has_side_effects=True, vmem_limit_bytes=VMEM_BYTES
        ),
        cost_estimate=pl.CostEstimate(
            flops=2 * n * rows * depth * (depth + 2 * n * rows),
            bytes_accessed=2 * depth * (depth + 2 * rows) + 4 * rows * rows,
            transcendentals=0,
        ),
    )(test_features, train_features, kernel_inverse)


def held_bytes(n, rows, depth):
    return 8 * n * rows * depth + 2 * depth * depth + 8 * n * rows * n * rows


def solution(mesh):
    in_specs = (P(("groups", "blk"), "panel"), P(("groups", "blk"), "panel"), P("panel", "blk"))
    out_specs = P(("groups", "panel"), "blk")
    blocks, panels = mesh.shape["blk"], mesh.shape["panel"]

    def run(test_features, train_features, kernel_inverse):
        rows, depth = test_features.shape
        same = train_features.shape == (rows, depth) and kernel_inverse.shape == (depth, depth)
        if blocks == 4 and panels == 4 and same and held_bytes(blocks, rows, depth) < VMEM_BYTES * 3 // 4:
            return fused(blocks, test_features, train_features, kernel_inverse)
        return local(test_features, train_features, kernel_inverse)

    return jax.shard_map(run, mesh=mesh, in_specs=in_specs, out_specs=out_specs, check_vma=False)
```

```python
import functools

import jax
import jax.numpy as jnp
from jax import lax
from jax.experimental import pallas as pl
from jax.experimental.pallas import tpu as pltpu
from jax.sharding import PartitionSpec as P

MESH = pl.DeviceIdType.MESH
VMEM_BYTES = 56 * 1024 * 1024


def local(test_features, train_features, kernel_inverse):
    all_rows = lax.all_gather(test_features, "blk", axis=0, tiled=True)
    slab_terms = jnp.dot(all_rows, kernel_inverse, preferred_element_type=jnp.float32)
    reduced = lax.psum_scatter(slab_terms, "panel", scatter_dimension=0, tiled=True).astype(
        jnp.bfloat16
    )
    preconditioned = lax.all_to_all(
        lax.all_to_all(reduced, "blk", split_axis=0, concat_axis=1, tiled=True),
        "panel",
        split_axis=1,
        concat_axis=0,
        tiled=True,
    )
    partial_scores = lax.dot_general(
        lax.all_gather(preconditioned, "blk", axis=0, tiled=True),
        train_features,
        (((1,), (1,)), ((), ())),
        preferred_element_type=jnp.float32,
    )
    blocks = lax.axis_size("blk")
    panels = lax.axis_size("panel")
    total_rows = partial_scores.shape[0]
    width = partial_scores.shape[1]
    grouped = partial_scores.reshape(blocks, panels, total_rows // (blocks * panels), width)
    partial_scores = jnp.transpose(grouped, (1, 0, 2, 3)).reshape(total_rows, width)
    return lax.psum_scatter(partial_scores, "panel", scatter_dimension=0, tiled=True)


def kernel(
    n, tile, t_ref, r_ref, k_ref, out_ref,
    tbuf, rbuf, stage, kbuf, pbuf, sbuf, crecv, xrecv, zrecv, fbuf, home,
    lsem, tsend, trecv, rsend, rrecv, gsend, grecv,
    csend, crsem, xsend, xrsem, zsend, zrsem, fsend, frsem,
):
    rows, depth = t_ref.shape
    half, quarter = rows // 2, rows // 4
    g = lax.axis_index("groups")
    b = lax.axis_index("blk")
    p = lax.axis_index("panel")
    core, chip = lax.rem(p, 2), p // 2
    sib = p + 1 - 2 * core
    peer = lax.rem(p + 2, 4)
    far = peer + 1 - 2 * core

    def at(blk, panel):
        return (g, blk, panel)

    def remote(src, dst, send, recv, blk, panel):
        return pltpu.make_async_remote_copy(
            src_ref=src, dst_ref=dst, send_sem=send, recv_sem=recv,
            device_id=at(blk, panel), device_id_type=MESH,
        )

    def on(condition, f, *args):
        @pl.when(condition)
        def _():
            f(*args)

    def both(*conditions):
        return functools.reduce(jnp.logical_and, conditions)

    barrier = pltpu.get_barrier_semaphore()
    partners = [at(lax.rem(b + k, n), p) for k in range(1, n)]
    partners += [at(b, sib), at(b, peer), at(b, far)]
    for partner in partners:
        pl.semaphore_signal(barrier, inc=1, device_id=partner, device_id_type=MESH)
    load_k = pltpu.make_async_copy(k_ref, kbuf, lsem.at[0])
    load_t = pltpu.make_async_copy(t_ref, tbuf.at[b], lsem.at[1])
    load_r = pltpu.make_async_copy(r_ref, rbuf.at[b], lsem.at[2])
    pl.semaphore_wait(barrier, n + 2)

    diag = b == p
    across = b == peer
    entry = jnp.logical_or(diag, across)
    top = pl.ds(0, half)
    low = pl.ds(half, half)

    own_top = remote(r_ref.at[top], rbuf.at[b, top], rsend.at[0], rrecv.at[b, 0], p, p)
    own_low = remote(r_ref.at[low], stage, rsend.at[1], grecv, b, peer)
    own_peer = remote(r_ref, rbuf.at[b], rsend.at[0], rrecv.at[b, 0], b, peer)
    own_sib = remote(r_ref, rbuf.at[b], rsend.at[1], rrecv.at[b, 0], b, sib)
    peer_sib = remote(rbuf.at[b], rbuf.at[b], rsend.at[2], rrecv.at[b, 0], b, sib)
    on(jnp.logical_not(diag), own_low.start)
    on(jnp.logical_not(diag), own_top.start)
    on(diag, own_peer.start)
    on(diag, own_sib.start)

    left, right = lax.rem(b + n - 1, n), lax.rem(b + 1, n)

    def t_copy(src, c, way):
        return remote(src, tbuf.at[c], tsend.at[way, c], trecv.at[c], right if way else left, p)

    on(b > 0, t_copy(t_ref, b, 0).start)
    on(b < n - 1, t_copy(t_ref, b, 1).start)
    load_t.start()
    load_k.start()
    on(diag, load_r.start)

    go_on = remote(stage, rbuf.at[b, low], gsend, rrecv.at[b, 1], peer, p)

    @pl.when(jnp.logical_not(across))
    def _():
        own_low.wait_recv()
        go_on.start()

    mine = jnp.where(diag, 0, 1)

    def r_move(j, which, way):
        part = rbuf.at[j, pl.ds(pl.multiple_of(which * half, half), half)]
        to = peer if way == 0 else sib
        return remote(part, part, rsend.at[3 + j * 3 + way], rrecv.at[j, which], b, to)

    def arrivals(k):
        def arrive(c, way, more):
            t_copy(tbuf.at[c], c, way).wait_recv()
            on(more, t_copy(tbuf.at[c], c, way).start)

        on(b - k >= 0, arrive, b - k, 1, b < n - 1)
        on(b + k < n, arrive, b + k, 0, b > 0)

    def across_arrives():
        own_peer.wait_recv()
        peer_sib.start()

    def z_half(j):
        r_move(j, mine, 0).wait_recv()
        r_move(j, mine, 0).start()
        r_move(j, mine, 1).start()

    def x_half(j):
        r_move(j, 1 - mine, 0).wait_recv()
        r_move(j, 1 - mine, 2).start()

    near = [lax.rem(b + k, n) for k in (1, n - 1, 2)]

    def condition(c):
        def step(t, carry):
            cols = pl.ds(pl.multiple_of(t * tile, tile), tile)
            part = jnp.dot(tbuf[c], kbuf[:, cols], preferred_element_type=jnp.float32)
            hi = part.astype(jnp.bfloat16)
            pbuf[c, :rows, cols] = hi
            pbuf[c, rows:, cols] = (part - hi.astype(jnp.float32)).astype(jnp.bfloat16)
            return carry

        lax.fori_loop(0, depth // tile, step, 0)

    def score(c):
        def step(j, carry):
            both_terms = lax.dot_general(
                pbuf[c], rbuf[j], (((1,), (1,)), ((), ())), preferred_element_type=jnp.float32
            )
            sbuf[c, j] = both_terms[:rows] + both_terms[rows:]
            return carry

        lax.fori_loop(0, n, step, 0)
        core_copy(c).start()

    def span(start, size):
        return pl.ds(pl.multiple_of(start, quarter), size)

    own_half = span(core * half, half)
    sib_half = span((1 - core) * half, half)
    own_part = span(core * half + chip * quarter, quarter)
    peer_part = span(core * half + (1 - chip) * quarter, quarter)

    def core_copy(c):
        return remote(sbuf.at[c, :, sib_half], crecv.at[c], csend.at[c], crsem.at[c], b, sib)

    def chip_copy(c):
        return remote(sbuf.at[c, :, peer_part], xrecv.at[c], xsend.at[c], xrsem.at[c], b, peer)

    def plane_copy(c, k):
        to = lax.rem(b + k, n)
        return remote(
            sbuf.at[c, to, own_part], zrecv.at[b, c], zsend.at[c, k - 1], zrsem.at[b, c], to, p
        )

    def join_cores(c):
        core_copy(c).wait_recv()
        sbuf[c, :, own_half] += crecv[c]
        chip_copy(c).start()

    def join_chips(c):
        chip_copy(c).wait_recv()
        sbuf[c, :, own_part] += xrecv[c]
        for k in range(1, n):
            plane_copy(c, k).start()

    def at_step(k, f):
        if k == 0:
            f(b)
        else:
            on(b - k >= 0, f, b - k)
            on(b + k < n, f, b + k)

    on(both(entry, across), across_arrives)

    @pl.when(entry)
    def _():
        for j in near:
            z_half(j)

    arrivals(1)

    @pl.when(entry)
    def _():
        for j in near:
            x_half(j)

    load_t.wait()
    load_k.wait()
    condition(b)
    at_step(1, condition)
    arrivals(2)
    at_step(2, condition)

    @pl.when(jnp.logical_not(entry))
    def _():
        own_sib.wait_recv()
        for j in near:
            r_move(j, 0, 1).wait_recv()
            r_move(j, 1, 1).wait_recv()

    on(diag, load_r.wait)
    for k in range(n):
        if k > 2:
            arrivals(k)
            at_step(k, condition)
        at_step(k, score)
        at_step(k, join_cores)
        if k > 0:
            at_step(k - 1, join_chips)
    at_step(n - 1, join_chips)

    def home_copy(c):
        return remote(fbuf.at[c], home.at[p], fsend.at[c], frsem.at[p], b, c)

    for c in range(n):
        total = sbuf[c, b, own_part]
        for k in range(1, n):
            j = lax.rem(b + k, n)
            remote(zrecv.at[j, c], zrecv.at[j, c], zsend.at[c, 0], zrsem.at[j, c], j, p).wait_recv()
            total = total + zrecv[j, c]
        fbuf[c] = total
        on(p != c, home_copy(c).start)
    out_ref[own_part, :] = fbuf[p]
    for q in range(n):
        @pl.when(p != q)
        def _():
            remote(home.at[q], home.at[q], fsend.at[q], frsem.at[q], b, q).wait_recv()
            start = (q % 2) * half + (q // 2) * quarter
            out_ref[start:start + quarter, :] = home[q]

    on(jnp.logical_not(diag), own_top.wait_send)
    on(jnp.logical_not(diag), own_low.wait_send)
    on(diag, own_peer.wait_send)
    on(diag, own_sib.wait_send)
    on(b > 0, t_copy(t_ref, b, 0).wait_send)
    on(b < n - 1, t_copy(t_ref, b, 1).wait_send)
    on(jnp.logical_not(across), go_on.wait_send)
    on(across, peer_sib.wait_send)

    @pl.when(entry)
    def _():
        for j in near:
            for way in range(2):
                r_move(j, mine, way).wait_send()
            r_move(j, 1 - mine, 2).wait_send()

    for k in range(1, n):
        on(both(b - k >= 0, b < n - 1), t_copy(tbuf.at[b - k], b - k, 1).wait_send)
        on(both(b + k < n, b > 0), t_copy(tbuf.at[b + k], b + k, 0).wait_send)
    for c in range(n):
        core_copy(c).wait_send()
        chip_copy(c).wait_send()
        for k in range(1, n):
            plane_copy(c, k).wait_send()
        on(p != c, home_copy(c).wait_send)


def fused(n, test_features, train_features, kernel_inverse):
    rows, depth = test_features.shape
    bf16, f32 = jnp.bfloat16, jnp.float32
    dma = pltpu.SemaphoreType.DMA
    return pl.pallas_call(
        functools.partial(kernel, n, min(512, depth)),
        out_shape=jax.ShapeDtypeStruct((rows, rows), f32),
        in_specs=[pl.BlockSpec(memory_space=pl.ANY)] * 3,
        out_specs=pl.BlockSpec(memory_space=pltpu.VMEM),
        scratch_shapes=[
            pltpu.VMEM((n, rows, depth), bf16),
            pltpu.VMEM((n, rows, depth), bf16),
            pltpu.VMEM((rows // 2, depth), bf16),
            pltpu.VMEM((depth, depth), bf16),
            pltpu.VMEM((n, 2 * rows, depth), bf16),
            pltpu.VMEM((n, n, rows, rows), f32),
            pltpu.VMEM((n, n, rows // 2, rows), f32),
            pltpu.VMEM((n, n, rows // 4, rows), f32),
            pltpu.VMEM((n, n, rows // 4, rows), f32),
            pltpu.VMEM((n, rows // 4, rows), f32),
            pltpu.VMEM((n, rows // 4, rows), f32),
            dma((3,)),
            dma((2, n)),
            dma((n,)),
            dma((3 + 3 * n,)),
            dma((n, 2)),
            dma,
            dma,
            dma((n,)),
            dma((n,)),
            dma((n,)),
            dma((n,)),
            dma((n, n - 1)),
            dma((n, n)),
            dma((n,)),
            dma((n,)),
        ],
        compiler_params=pltpu.CompilerParams(
            collective_id=0, has_side_effects=True, vmem_limit_bytes=VMEM_BYTES
        ),
        cost_estimate=pl.CostEstimate(
            flops=2 * n * rows * depth * (depth + 2 * n * rows),
            bytes_accessed=2 * depth * (depth + 2 * rows) + 4 * rows * rows,
            transcendentals=0,
        ),
    )(test_features, train_features, kernel_inverse)


def held_bytes(n, rows, depth):
    return 8 * n * rows * depth + 2 * depth * depth + 8 * n * rows * n * rows


def solution(mesh):
    in_specs = (P(("groups", "blk"), "panel"), P(("groups", "blk"), "panel"), P("panel", "blk"))
    out_specs = P(("groups", "panel"), "blk")
    blocks, panels = mesh.shape["blk"], mesh.shape["panel"]

    def run(test_features, train_features, kernel_inverse):
        rows, depth = test_features.shape
        same = train_features.shape == (rows, depth) and kernel_inverse.shape == (depth, depth)
        if blocks == 4 and panels == 4 and same and held_bytes(blocks, rows, depth) < VMEM_BYTES * 3 // 4:
            return fused(blocks, test_features, train_features, kernel_inverse)
        return local(test_features, train_features, kernel_inverse)

    return jax.shard_map(run, mesh=mesh, in_specs=in_specs, out_specs=out_specs, check_vma=False)
```

```python
import functools

import jax
import jax.numpy as jnp
from jax import lax
from jax.experimental import pallas as pl
from jax.experimental.pallas import tpu as pltpu
from jax.sharding import PartitionSpec as P

MESH = pl.DeviceIdType.MESH
VMEM_BYTES = 56 * 1024 * 1024


def local(test_features, train_features, kernel_inverse):
    all_rows = lax.all_gather(test_features, "blk", axis=0, tiled=True)
    slab_terms = jnp.dot(all_rows, kernel_inverse, preferred_element_type=jnp.float32)
    reduced = lax.psum_scatter(slab_terms, "panel", scatter_dimension=0, tiled=True).astype(
        jnp.bfloat16
    )
    preconditioned = lax.all_to_all(
        lax.all_to_all(reduced, "blk", split_axis=0, concat_axis=1, tiled=True),
        "panel",
        split_axis=1,
        concat_axis=0,
        tiled=True,
    )
    partial_scores = lax.dot_general(
        lax.all_gather(preconditioned, "blk", axis=0, tiled=True),
        train_features,
        (((1,), (1,)), ((), ())),
        preferred_element_type=jnp.float32,
    )
    blocks = lax.axis_size("blk")
    panels = lax.axis_size("panel")
    total_rows = partial_scores.shape[0]
    width = partial_scores.shape[1]
    grouped = partial_scores.reshape(blocks, panels, total_rows // (blocks * panels), width)
    partial_scores = jnp.transpose(grouped, (1, 0, 2, 3)).reshape(total_rows, width)
    return lax.psum_scatter(partial_scores, "panel", scatter_dimension=0, tiled=True)


def kernel(
    n, tile, t_ref, r_ref, k_ref, out_ref,
    tbuf, rbuf, stage, kbuf, pbuf, sbuf, crecv, xout, xrecv, zout, zrecv, fbuf, home,
    lsem, tsend, trecv, rsend, rrecv, gsend, grecv,
    csend, crsem, xsend, xrsem, zsend, zrsem, fsend, frsem,
):
    rows, depth = t_ref.shape
    half, quarter = rows // 2, rows // 4
    g = lax.axis_index("groups")
    b = lax.axis_index("blk")
    p = lax.axis_index("panel")
    core, chip = lax.rem(p, 2), p // 2
    sib = p + 1 - 2 * core
    peer = lax.rem(p + 2, 4)
    far = peer + 1 - 2 * core

    def at(blk, panel):
        return (g, blk, panel)

    def remote(src, dst, send, recv, blk, panel):
        return pltpu.make_async_remote_copy(
            src_ref=src, dst_ref=dst, send_sem=send, recv_sem=recv,
            device_id=at(blk, panel), device_id_type=MESH,
        )

    def on(condition, f, *args):
        @pl.when(condition)
        def _():
            f(*args)

    def both(*conditions):
        return functools.reduce(jnp.logical_and, conditions)

    barrier = pltpu.get_barrier_semaphore()
    partners = [at(lax.rem(b + k, n), p) for k in range(1, n)]
    partners += [at(b, sib), at(b, peer), at(b, far)]
    for partner in partners:
        pl.semaphore_signal(barrier, inc=1, device_id=partner, device_id_type=MESH)
    load_k = pltpu.make_async_copy(k_ref, kbuf, lsem.at[0])
    load_t = pltpu.make_async_copy(t_ref, tbuf.at[b], lsem.at[1])
    load_r = pltpu.make_async_copy(r_ref, rbuf.at[b], lsem.at[2])
    pl.semaphore_wait(barrier, n + 2)

    diag = b == p
    across = b == peer
    entry = jnp.logical_or(diag, across)
    top = pl.ds(0, half)
    low = pl.ds(half, half)

    own_top = remote(r_ref.at[top], rbuf.at[b, top], rsend.at[0], rrecv.at[b, 0], p, p)
    own_low = remote(r_ref.at[low], stage, rsend.at[1], grecv, b, peer)
    own_peer = remote(r_ref, rbuf.at[b], rsend.at[0], rrecv.at[b, 0], b, peer)
    own_sib = remote(r_ref, rbuf.at[b], rsend.at[1], rrecv.at[b, 0], b, sib)
    peer_sib = remote(rbuf.at[b], rbuf.at[b], rsend.at[2], rrecv.at[b, 0], b, sib)
    on(jnp.logical_not(diag), own_low.start)
    on(jnp.logical_not(diag), own_top.start)
    on(diag, own_peer.start)
    on(diag, own_sib.start)

    left, right = lax.rem(b + n - 1, n), lax.rem(b + 1, n)

    def t_copy(src, c, way):
        return remote(src, tbuf.at[c], tsend.at[way, c], trecv.at[c], right if way else left, p)

    on(b > 0, t_copy(t_ref, b, 0).start)
    on(b < n - 1, t_copy(t_ref, b, 1).start)
    load_t.start()
    load_k.start()
    on(diag, load_r.start)

    go_on = remote(stage, rbuf.at[b, low], gsend, rrecv.at[b, 1], peer, p)

    @pl.when(jnp.logical_not(across))
    def _():
        own_low.wait_recv()
        go_on.start()

    mine = jnp.where(diag, 0, 1)

    def r_move(j, which, way):
        part = rbuf.at[j, pl.ds(pl.multiple_of(which * half, half), half)]
        to = peer if way == 0 else sib
        return remote(part, part, rsend.at[3 + j * 3 + way], rrecv.at[j, which], b, to)

    def arrivals(k):
        def arrive(c, way, more):
            t_copy(tbuf.at[c], c, way).wait_recv()
            on(more, t_copy(tbuf.at[c], c, way).start)

        on(b - k >= 0, arrive, b - k, 1, b < n - 1)
        on(b + k < n, arrive, b + k, 0, b > 0)

    def across_arrives():
        own_peer.wait_recv()
        peer_sib.start()

    def z_half(j):
        r_move(j, mine, 0).wait_recv()
        r_move(j, mine, 0).start()
        r_move(j, mine, 1).start()

    def x_half(j):
        r_move(j, 1 - mine, 0).wait_recv()
        r_move(j, 1 - mine, 2).start()

    near = [lax.rem(b + k, n) for k in (1, n - 1, 2)]

    def condition(c):
        def step(t, carry):
            cols = pl.ds(pl.multiple_of(t * tile, tile), tile)
            part = jnp.dot(tbuf[c], kbuf[:, cols], preferred_element_type=jnp.float32)
            hi = part.astype(jnp.bfloat16)
            pbuf[c, :rows, cols] = hi
            pbuf[c, rows:, cols] = (part - hi.astype(jnp.float32)).astype(jnp.bfloat16)
            return carry

        lax.fori_loop(0, depth // tile, step, 0)

    def score(c):
        def step(j, carry):
            both_terms = lax.dot_general(
                pbuf[c], rbuf[j], (((1,), (1,)), ((), ())), preferred_element_type=jnp.float32
            )
            sbuf[c, j] = both_terms[:rows] + both_terms[rows:]
            return carry

        lax.fori_loop(0, n, step, 0)
        core_copy(c).start()

    def span(start, size):
        return pl.ds(pl.multiple_of(start, quarter), size)

    own_half = span(core * half, half)
    sib_half = span((1 - core) * half, half)
    own_part = span(core * half + chip * quarter, quarter)
    peer_part = span(core * half + (1 - chip) * quarter, quarter)

    def core_copy(c):
        return remote(sbuf.at[c, :, sib_half], crecv.at[c], csend.at[c], crsem.at[c], b, sib)

    def chip_copy(c):
        return remote(xout.at[c], xrecv.at[c], xsend.at[c], xrsem.at[c], b, peer)

    def plane_copy(c, k):
        to = lax.rem(b + k, n)
        return remote(
            zout.at[c, to], zrecv.at[b, c], zsend.at[c, k - 1], zrsem.at[b, c], to, p
        )

    def join_cores(c):
        core_copy(c).wait_recv()
        sbuf[c, :, own_half] += crecv[c]
        xout[c] = sbuf[c, :, peer_part].astype(xout.dtype)
        chip_copy(c).start()

    def join_chips(c):
        chip_copy(c).wait_recv()
        total = sbuf[c, :, own_part] + xrecv[c].astype(jnp.float32)
        sbuf[c, :, own_part] = total
        zout[c] = total.astype(zout.dtype)
        for k in range(1, n):
            plane_copy(c, k).start()

    def at_step(k, f):
        if k == 0:
            f(b)
        else:
            on(b - k >= 0, f, b - k)
            on(b + k < n, f, b + k)

    on(across, across_arrives)
    arrivals(1)

    @pl.when(entry)
    def _():
        for j in near:
            z_half(j)

    load_t.wait()
    load_k.wait()
    condition(b)
    arrivals(2)

    @pl.when(entry)
    def _():
        for j in near:
            x_half(j)

    at_step(1, condition)
    at_step(2, condition)

    @pl.when(jnp.logical_not(entry))
    def _():
        own_sib.wait_recv()
        for j in near:
            r_move(j, 0, 1).wait_recv()
            r_move(j, 1, 1).wait_recv()

    on(diag, load_r.wait)
    for k in range(n):
        if k > 2:
            arrivals(k)
            at_step(k, condition)
        at_step(k, score)
        at_step(k, join_cores)
        if k > 0:
            at_step(k - 1, join_chips)
    at_step(n - 1, join_chips)

    def home_copy(c):
        return remote(fbuf.at[c], home.at[p], fsend.at[c], frsem.at[p], b, c)

    for c in range(n):
        total = sbuf[c, b, own_part]
        for k in range(1, n):
            j = lax.rem(b + k, n)
            remote(zrecv.at[j, c], zrecv.at[j, c], zsend.at[c, 0], zrsem.at[j, c], j, p).wait_recv()
            total = total + zrecv[j, c].astype(jnp.float32)
        fbuf[c] = total
        on(p != c, home_copy(c).start)
    out_ref[own_part, :] = fbuf[p]
    for q in range(n):
        @pl.when(p != q)
        def _():
            remote(home.at[q], home.at[q], fsend.at[q], frsem.at[q], b, q).wait_recv()
            start = (q % 2) * half + (q // 2) * quarter
            out_ref[start:start + quarter, :] = home[q]

    on(jnp.logical_not(diag), own_top.wait_send)
    on(jnp.logical_not(diag), own_low.wait_send)
    on(diag, own_peer.wait_send)
    on(diag, own_sib.wait_send)
    on(b > 0, t_copy(t_ref, b, 0).wait_send)
    on(b < n - 1, t_copy(t_ref, b, 1).wait_send)
    on(jnp.logical_not(across), go_on.wait_send)
    on(across, peer_sib.wait_send)

    @pl.when(entry)
    def _():
        for j in near:
            for way in range(2):
                r_move(j, mine, way).wait_send()
            r_move(j, 1 - mine, 2).wait_send()

    for k in range(1, n):
        on(both(b - k >= 0, b < n - 1), t_copy(tbuf.at[b - k], b - k, 1).wait_send)
        on(both(b + k < n, b > 0), t_copy(tbuf.at[b + k], b + k, 0).wait_send)
    for c in range(n):
        core_copy(c).wait_send()
        chip_copy(c).wait_send()
        for k in range(1, n):
            plane_copy(c, k).wait_send()
        on(p != c, home_copy(c).wait_send)


def fused(n, test_features, train_features, kernel_inverse):
    rows, depth = test_features.shape
    bf16, f32 = jnp.bfloat16, jnp.float32
    dma = pltpu.SemaphoreType.DMA
    return pl.pallas_call(
        functools.partial(kernel, n, min(512, depth)),
        out_shape=jax.ShapeDtypeStruct((rows, rows), f32),
        in_specs=[pl.BlockSpec(memory_space=pl.ANY)] * 3,
        out_specs=pl.BlockSpec(memory_space=pltpu.VMEM),
        scratch_shapes=[
            pltpu.VMEM((n, rows, depth), bf16),
            pltpu.VMEM((n, rows, depth), bf16),
            pltpu.VMEM((rows // 2, depth), bf16),
            pltpu.VMEM((depth, depth), bf16),
            pltpu.VMEM((n, 2 * rows, depth), bf16),
            pltpu.VMEM((n, n, rows, rows), f32),
            pltpu.VMEM((n, n, rows // 2, rows), f32),
            pltpu.VMEM((n, n, rows // 4, rows), bf16),
            pltpu.VMEM((n, n, rows // 4, rows), bf16),
            pltpu.VMEM((n, n, rows // 4, rows), bf16),
            pltpu.VMEM((n, n, rows // 4, rows), bf16),
            pltpu.VMEM((n, rows // 4, rows), f32),
            pltpu.VMEM((n, rows // 4, rows), f32),
            dma((3,)),
            dma((2, n)),
            dma((n,)),
            dma((3 + 3 * n,)),
            dma((n, 2)),
            dma,
            dma,
            dma((n,)),
            dma((n,)),
            dma((n,)),
            dma((n,)),
            dma((n, n - 1)),
            dma((n, n)),
            dma((n,)),
            dma((n,)),
        ],
        compiler_params=pltpu.CompilerParams(
            collective_id=0, has_side_effects=True, vmem_limit_bytes=VMEM_BYTES
        ),
        cost_estimate=pl.CostEstimate(
            flops=2 * n * rows * depth * (depth + 2 * n * rows),
            bytes_accessed=2 * depth * (depth + 2 * rows) + 4 * rows * rows,
            transcendentals=0,
        ),
    )(test_features, train_features, kernel_inverse)


def held_bytes(n, rows, depth):
    return 8 * n * rows * depth + 2 * depth * depth + 8 * n * rows * n * rows


def solution(mesh):
    in_specs = (P(("groups", "blk"), "panel"), P(("groups", "blk"), "panel"), P("panel", "blk"))
    out_specs = P(("groups", "panel"), "blk")
    blocks, panels = mesh.shape["blk"], mesh.shape["panel"]

    def run(test_features, train_features, kernel_inverse):
        rows, depth = test_features.shape
        same = train_features.shape == (rows, depth) and kernel_inverse.shape == (depth, depth)
        if blocks == 4 and panels == 4 and same and held_bytes(blocks, rows, depth) < VMEM_BYTES * 3 // 4:
            return fused(blocks, test_features, train_features, kernel_inverse)
        return local(test_features, train_features, kernel_inverse)

    return jax.shard_map(run, mesh=mesh, in_specs=in_specs, out_specs=out_specs, check_vma=False)
```

```python
import functools

import jax
import jax.numpy as jnp
from jax import lax
from jax.experimental import pallas as pl
from jax.experimental.pallas import tpu as pltpu
from jax.sharding import PartitionSpec as P

MESH = pl.DeviceIdType.MESH
VMEM_BYTES = 56 * 1024 * 1024


def local(test_features, train_features, kernel_inverse):
    all_rows = lax.all_gather(test_features, "blk", axis=0, tiled=True)
    slab_terms = jnp.dot(all_rows, kernel_inverse, preferred_element_type=jnp.float32)
    reduced = lax.psum_scatter(slab_terms, "panel", scatter_dimension=0, tiled=True).astype(
        jnp.bfloat16
    )
    preconditioned = lax.all_to_all(
        lax.all_to_all(reduced, "blk", split_axis=0, concat_axis=1, tiled=True),
        "panel",
        split_axis=1,
        concat_axis=0,
        tiled=True,
    )
    partial_scores = lax.dot_general(
        lax.all_gather(preconditioned, "blk", axis=0, tiled=True),
        train_features,
        (((1,), (1,)), ((), ())),
        preferred_element_type=jnp.float32,
    )
    blocks = lax.axis_size("blk")
    panels = lax.axis_size("panel")
    total_rows = partial_scores.shape[0]
    width = partial_scores.shape[1]
    grouped = partial_scores.reshape(blocks, panels, total_rows // (blocks * panels), width)
    partial_scores = jnp.transpose(grouped, (1, 0, 2, 3)).reshape(total_rows, width)
    return lax.psum_scatter(partial_scores, "panel", scatter_dimension=0, tiled=True)


def kernel(
    n, tile, t_ref, r_ref, k_ref, out_ref,
    tbuf, rbuf, stage, kbuf, pbuf, sbuf, crecv, xout, xrecv, zout, zrecv, fbuf, home,
    lsem, tsend, trecv, rsend, rrecv, gsend, grecv,
    csend, crsem, xsend, xrsem, zsend, zrsem, fsend, frsem,
):
    rows, depth = t_ref.shape
    half, quarter = rows // 2, rows // 4
    g = lax.axis_index("groups")
    b = lax.axis_index("blk")
    p = lax.axis_index("panel")
    core, chip = lax.rem(p, 2), p // 2
    sib = p + 1 - 2 * core
    peer = lax.rem(p + 2, 4)
    far = peer + 1 - 2 * core

    def at(blk, panel):
        return (g, blk, panel)

    def remote(src, dst, send, recv, blk, panel):
        return pltpu.make_async_remote_copy(
            src_ref=src, dst_ref=dst, send_sem=send, recv_sem=recv,
            device_id=at(blk, panel), device_id_type=MESH,
        )

    def on(condition, f, *args):
        @pl.when(condition)
        def _():
            f(*args)

    def both(*conditions):
        return functools.reduce(jnp.logical_and, conditions)

    barrier = pltpu.get_barrier_semaphore()
    partners = [at(lax.rem(b + k, n), p) for k in range(1, n)]
    partners += [at(b, sib), at(b, peer), at(b, far)]
    for partner in partners:
        pl.semaphore_signal(barrier, inc=1, device_id=partner, device_id_type=MESH)
    load_k = pltpu.make_async_copy(k_ref, kbuf, lsem.at[0])
    load_t = pltpu.make_async_copy(t_ref, tbuf.at[b], lsem.at[1])
    load_r = pltpu.make_async_copy(r_ref, rbuf.at[b], lsem.at[2])
    pl.semaphore_wait(barrier, n + 2)

    diag = b == p
    across = b == peer
    entry = jnp.logical_or(diag, across)
    top = pl.ds(0, half)
    low = pl.ds(half, half)

    own_top = remote(r_ref.at[top], rbuf.at[b, top], rsend.at[0], rrecv.at[b, 0], p, p)
    own_low = remote(r_ref.at[low], stage, rsend.at[1], grecv, b, peer)
    own_peer = remote(r_ref, rbuf.at[b], rsend.at[0], rrecv.at[b, 0], b, peer)
    own_sib = remote(r_ref, rbuf.at[b], rsend.at[1], rrecv.at[b, 0], b, sib)
    peer_sib = remote(rbuf.at[b], rbuf.at[b], rsend.at[2], rrecv.at[b, 0], b, sib)
    on(jnp.logical_not(diag), own_low.start)
    on(diag, own_peer.start)
    on(diag, own_sib.start)

    left, right = lax.rem(b + n - 1, n), lax.rem(b + 1, n)

    def t_copy(src, c, way, part):
        to = right if way else left
        rows_of = low if part else top
        return remote(
            src.at[rows_of], tbuf.at[c, rows_of], tsend.at[way, c, part], trecv.at[c, part], to, p
        )

    for part in (0, 1):
        on(b > 0, t_copy(t_ref, b, 0, part).start)
        on(b < n - 1, t_copy(t_ref, b, 1, part).start)
    on(jnp.logical_not(diag), own_top.start)
    load_t.start()
    load_k.start()
    on(diag, load_r.start)

    go_on = remote(stage, rbuf.at[b, low], gsend, rrecv.at[b, 1], peer, p)

    @pl.when(jnp.logical_not(across))
    def _():
        own_low.wait_recv()
        go_on.start()

    mine = jnp.where(diag, 0, 1)

    def r_move(j, which, way):
        part = rbuf.at[j, pl.ds(pl.multiple_of(which * half, half), half)]
        to = peer if way == 0 else sib
        return remote(part, part, rsend.at[3 + j * 3 + way], rrecv.at[j, which], b, to)

    def arrivals(k):
        def arrive(c, way, more):
            for part in (0, 1):
                t_copy(tbuf.at[c], c, way, part).wait_recv()
                on(more, t_copy(tbuf.at[c], c, way, part).start)

        on(b - k >= 0, arrive, b - k, 1, b < n - 1)
        on(b + k < n, arrive, b + k, 0, b > 0)

    def across_arrives():
        own_peer.wait_recv()
        peer_sib.start()

    def z_half(j):
        r_move(j, mine, 0).wait_recv()
        r_move(j, mine, 0).start()
        r_move(j, mine, 1).start()

    def x_half(j):
        r_move(j, 1 - mine, 0).wait_recv()
        r_move(j, 1 - mine, 2).start()

    near = [lax.rem(b + k, n) for k in (1, n - 1, 2)]

    def condition(c):
        def step(t, carry):
            cols = pl.ds(pl.multiple_of(t * tile, tile), tile)
            part = jnp.dot(tbuf[c], kbuf[:, cols], preferred_element_type=jnp.float32)
            hi = part.astype(jnp.bfloat16)
            pbuf[c, :rows, cols] = hi
            pbuf[c, rows:, cols] = (part - hi.astype(jnp.float32)).astype(jnp.bfloat16)
            return carry

        lax.fori_loop(0, depth // tile, step, 0)

    def score(c):
        def step(j, carry):
            both_terms = lax.dot_general(
                pbuf[c], rbuf[j], (((1,), (1,)), ((), ())), preferred_element_type=jnp.float32
            )
            sbuf[c, j] = both_terms[:rows] + both_terms[rows:]
            return carry

        lax.fori_loop(0, n, step, 0)
        core_copy(c).start()

    def span(start, size):
        return pl.ds(pl.multiple_of(start, quarter), size)

    own_half = span(core * half, half)
    sib_half = span((1 - core) * half, half)
    own_part = span(core * half + chip * quarter, quarter)
    peer_part = span(core * half + (1 - chip) * quarter, quarter)

    def core_copy(c):
        return remote(sbuf.at[c, :, sib_half], crecv.at[c], csend.at[c], crsem.at[c], b, sib)

    def chip_copy(c):
        return remote(xout.at[c], xrecv.at[c], xsend.at[c], xrsem.at[c], b, peer)

    def plane_copy(c, k):
        to = lax.rem(b + k, n)
        return remote(
            zout.at[c, to], zrecv.at[b, c], zsend.at[c, k - 1], zrsem.at[b, c], to, p
        )

    def join_cores(c):
        core_copy(c).wait_recv()
        sbuf[c, :, own_half] += crecv[c]
        xout[c] = sbuf[c, :, peer_part].astype(xout.dtype)
        chip_copy(c).start()

    def join_chips(c):
        chip_copy(c).wait_recv()
        total = sbuf[c, :, own_part] + xrecv[c].astype(jnp.float32)
        sbuf[c, :, own_part] = total
        zout[c] = total.astype(zout.dtype)
        for k in range(1, n):
            plane_copy(c, k).start()

    def at_step(k, f):
        if k == 0:
            f(b)
        else:
            on(b - k >= 0, f, b - k)
            on(b + k < n, f, b + k)

    on(across, across_arrives)
    arrivals(1)

    @pl.when(entry)
    def _():
        for j in near:
            z_half(j)

    load_t.wait()
    load_k.wait()
    condition(b)
    arrivals(2)

    @pl.when(entry)
    def _():
        for j in near:
            x_half(j)

    at_step(1, condition)
    at_step(2, condition)

    @pl.when(jnp.logical_not(entry))
    def _():
        own_sib.wait_recv()
        for j in near:
            r_move(j, 0, 1).wait_recv()
            r_move(j, 1, 1).wait_recv()

    on(diag, load_r.wait)
    for k in range(n):
        if k > 2:
            arrivals(k)
            at_step(k, condition)
        at_step(k, score)
        at_step(k, join_cores)
        if k > 0:
            at_step(k - 1, join_chips)
    at_step(n - 1, join_chips)

    def home_copy(c):
        return remote(fbuf.at[c], home.at[p], fsend.at[c], frsem.at[p], b, c)

    for c in range(n):
        total = sbuf[c, b, own_part]
        for k in range(1, n):
            j = lax.rem(b + k, n)
            remote(zrecv.at[j, c], zrecv.at[j, c], zsend.at[c, 0], zrsem.at[j, c], j, p).wait_recv()
            total = total + zrecv[j, c].astype(jnp.float32)
        fbuf[c] = total
        on(p != c, home_copy(c).start)
    out_ref[own_part, :] = fbuf[p]
    for q in range(n):
        @pl.when(p != q)
        def _():
            remote(home.at[q], home.at[q], fsend.at[q], frsem.at[q], b, q).wait_recv()
            start = (q % 2) * half + (q // 2) * quarter
            out_ref[start:start + quarter, :] = home[q]

    on(jnp.logical_not(diag), own_top.wait_send)
    on(jnp.logical_not(diag), own_low.wait_send)
    on(diag, own_peer.wait_send)
    on(diag, own_sib.wait_send)
    for part in (0, 1):
        on(b > 0, t_copy(t_ref, b, 0, part).wait_send)
        on(b < n - 1, t_copy(t_ref, b, 1, part).wait_send)
    on(jnp.logical_not(across), go_on.wait_send)
    on(across, peer_sib.wait_send)

    @pl.when(entry)
    def _():
        for j in near:
            for way in range(2):
                r_move(j, mine, way).wait_send()
            r_move(j, 1 - mine, 2).wait_send()

    for k in range(1, n):
        for part in (0, 1):
            on(both(b - k >= 0, b < n - 1), t_copy(tbuf.at[b - k], b - k, 1, part).wait_send)
            on(both(b + k < n, b > 0), t_copy(tbuf.at[b + k], b + k, 0, part).wait_send)
    for c in range(n):
        core_copy(c).wait_send()
        chip_copy(c).wait_send()
        for k in range(1, n):
            plane_copy(c, k).wait_send()
        on(p != c, home_copy(c).wait_send)


def fused(n, test_features, train_features, kernel_inverse):
    rows, depth = test_features.shape
    bf16, f32 = jnp.bfloat16, jnp.float32
    dma = pltpu.SemaphoreType.DMA
    return pl.pallas_call(
        functools.partial(kernel, n, min(512, depth)),
        out_shape=jax.ShapeDtypeStruct((rows, rows), f32),
        in_specs=[pl.BlockSpec(memory_space=pl.ANY)] * 3,
        out_specs=pl.BlockSpec(memory_space=pltpu.VMEM),
        scratch_shapes=[
            pltpu.VMEM((n, rows, depth), bf16),
            pltpu.VMEM((n, rows, depth), bf16),
            pltpu.VMEM((rows // 2, depth), bf16),
            pltpu.VMEM((depth, depth), bf16),
            pltpu.VMEM((n, 2 * rows, depth), bf16),
            pltpu.VMEM((n, n, rows, rows), f32),
            pltpu.VMEM((n, n, rows // 2, rows), f32),
            pltpu.VMEM((n, n, rows // 4, rows), bf16),
            pltpu.VMEM((n, n, rows // 4, rows), bf16),
            pltpu.VMEM((n, n, rows // 4, rows), bf16),
            pltpu.VMEM((n, n, rows // 4, rows), bf16),
            pltpu.VMEM((n, rows // 4, rows), f32),
            pltpu.VMEM((n, rows // 4, rows), f32),
            dma((3,)),
            dma((2, n, 2)),
            dma((n, 2)),
            dma((3 + 3 * n,)),
            dma((n, 2)),
            dma,
            dma,
            dma((n,)),
            dma((n,)),
            dma((n,)),
            dma((n,)),
            dma((n, n - 1)),
            dma((n, n)),
            dma((n,)),
            dma((n,)),
        ],
        compiler_params=pltpu.CompilerParams(
            collective_id=0, has_side_effects=True, vmem_limit_bytes=VMEM_BYTES
        ),
        cost_estimate=pl.CostEstimate(
            flops=2 * n * rows * depth * (depth + 2 * n * rows),
            bytes_accessed=2 * depth * (depth + 2 * rows) + 4 * rows * rows,
            transcendentals=0,
        ),
    )(test_features, train_features, kernel_inverse)


def held_bytes(n, rows, depth):
    return 8 * n * rows * depth + 2 * depth * depth + 8 * n * rows * n * rows


def solution(mesh):
    in_specs = (P(("groups", "blk"), "panel"), P(("groups", "blk"), "panel"), P("panel", "blk"))
    out_specs = P(("groups", "panel"), "blk")
    blocks, panels = mesh.shape["blk"], mesh.shape["panel"]

    def run(test_features, train_features, kernel_inverse):
        rows, depth = test_features.shape
        same = train_features.shape == (rows, depth) and kernel_inverse.shape == (depth, depth)
        if blocks == 4 and panels == 4 and same and held_bytes(blocks, rows, depth) < VMEM_BYTES * 3 // 4:
            return fused(blocks, test_features, train_features, kernel_inverse)
        return local(test_features, train_features, kernel_inverse)

    return jax.shard_map(run, mesh=mesh, in_specs=in_specs, out_specs=out_specs, check_vma=False)
```

```python
import functools

import jax
import jax.numpy as jnp
from jax import lax
from jax.experimental import pallas as pl
from jax.experimental.pallas import tpu as pltpu
from jax.sharding import PartitionSpec as P

MESH = pl.DeviceIdType.MESH
VMEM_BYTES = 56 * 1024 * 1024


def local(test_features, train_features, kernel_inverse):
    all_rows = lax.all_gather(test_features, "blk", axis=0, tiled=True)
    slab_terms = jnp.dot(all_rows, kernel_inverse, preferred_element_type=jnp.float32)
    reduced = lax.psum_scatter(slab_terms, "panel", scatter_dimension=0, tiled=True).astype(
        jnp.bfloat16
    )
    preconditioned = lax.all_to_all(
        lax.all_to_all(reduced, "blk", split_axis=0, concat_axis=1, tiled=True),
        "panel",
        split_axis=1,
        concat_axis=0,
        tiled=True,
    )
    partial_scores = lax.dot_general(
        lax.all_gather(preconditioned, "blk", axis=0, tiled=True),
        train_features,
        (((1,), (1,)), ((), ())),
        preferred_element_type=jnp.float32,
    )
    blocks = lax.axis_size("blk")
    panels = lax.axis_size("panel")
    total_rows = partial_scores.shape[0]
    width = partial_scores.shape[1]
    grouped = partial_scores.reshape(blocks, panels, total_rows // (blocks * panels), width)
    partial_scores = jnp.transpose(grouped, (1, 0, 2, 3)).reshape(total_rows, width)
    return lax.psum_scatter(partial_scores, "panel", scatter_dimension=0, tiled=True)


def kernel(
    n, tile, t_ref, r_ref, k_ref, out_ref,
    tbuf, rbuf, stage, kbuf, pbuf, sbuf, crecv, xout, xrecv, zout, zrecv, fbuf, home,
    lsem, tsend, trecv, rsend, rrecv, gsend, grecv,
    csend, crsem, xsend, xrsem, zsend, zrsem, fsend, frsem,
):
    rows, depth = t_ref.shape
    half, quarter = rows // 2, rows // 4
    g = lax.axis_index("groups")
    b = lax.axis_index("blk")
    p = lax.axis_index("panel")
    core, chip = lax.rem(p, 2), p // 2
    sib = p + 1 - 2 * core
    peer = lax.rem(p + 2, 4)
    far = peer + 1 - 2 * core

    def at(blk, panel):
        return (g, blk, panel)

    def remote(src, dst, send, recv, blk, panel):
        return pltpu.make_async_remote_copy(
            src_ref=src, dst_ref=dst, send_sem=send, recv_sem=recv,
            device_id=at(blk, panel), device_id_type=MESH,
        )

    def on(condition, f, *args):
        @pl.when(condition)
        def _():
            f(*args)

    def both(*conditions):
        return functools.reduce(jnp.logical_and, conditions)

    barrier = pltpu.get_barrier_semaphore()
    partners = [at(lax.rem(b + k, n), p) for k in range(1, n)]
    partners += [at(b, sib), at(b, peer), at(b, far)]
    for partner in partners:
        pl.semaphore_signal(barrier, inc=1, device_id=partner, device_id_type=MESH)
    load_k = pltpu.make_async_copy(k_ref, kbuf, lsem.at[0])
    load_t = pltpu.make_async_copy(t_ref, tbuf.at[b], lsem.at[1])
    load_r = pltpu.make_async_copy(r_ref, rbuf.at[b], lsem.at[2])
    pl.semaphore_wait(barrier, n + 2)

    diag = b == p
    across = b == peer
    entry = jnp.logical_or(diag, across)
    top = pl.ds(0, half)
    low = pl.ds(half, half)

    own_top = remote(r_ref.at[top], rbuf.at[b, top], rsend.at[0], rrecv.at[b, 0], p, p)
    own_low = remote(r_ref.at[low], stage, rsend.at[1], grecv, b, peer)
    own_peer = remote(r_ref, rbuf.at[b], rsend.at[0], rrecv.at[b, 0], b, peer)
    own_sib = remote(r_ref, rbuf.at[b], rsend.at[1], rrecv.at[b, 0], b, sib)
    peer_sib = remote(rbuf.at[b], rbuf.at[b], rsend.at[2], rrecv.at[b, 0], b, sib)
    on(jnp.logical_not(diag), own_low.start)
    on(diag, own_peer.start)
    on(diag, own_sib.start)

    left, right = lax.rem(b + n - 1, n), lax.rem(b + 1, n)

    def t_copy(src, c, way, part):
        to = right if way else left
        rows_of = pl.ds(part * quarter, quarter)
        return remote(
            src.at[rows_of], tbuf.at[c, rows_of], tsend.at[way, c, part], trecv.at[c, part], to, p
        )

    for part in range(4):
        on(b > 0, t_copy(t_ref, b, 0, part).start)
        on(b < n - 1, t_copy(t_ref, b, 1, part).start)
    on(jnp.logical_not(diag), own_top.start)
    load_t.start()
    load_k.start()
    on(diag, load_r.start)

    go_on = remote(stage, rbuf.at[b, low], gsend, rrecv.at[b, 1], peer, p)

    @pl.when(jnp.logical_not(across))
    def _():
        own_low.wait_recv()
        go_on.start()

    mine = jnp.where(diag, 0, 1)

    def r_move(j, which, way):
        part = rbuf.at[j, pl.ds(pl.multiple_of(which * half, half), half)]
        to = peer if way == 0 else sib
        return remote(part, part, rsend.at[3 + j * 3 + way], rrecv.at[j, which], b, to)

    def arrivals(k):
        def arrive(c, way, more):
            for part in range(4):
                t_copy(tbuf.at[c], c, way, part).wait_recv()
                on(more, t_copy(tbuf.at[c], c, way, part).start)

        on(b - k >= 0, arrive, b - k, 1, b < n - 1)
        on(b + k < n, arrive, b + k, 0, b > 0)

    def across_arrives():
        own_peer.wait_recv()
        peer_sib.start()

    def z_half(j):
        r_move(j, mine, 0).wait_recv()
        r_move(j, mine, 0).start()
        r_move(j, mine, 1).start()

    def x_half(j):
        r_move(j, 1 - mine, 0).wait_recv()
        r_move(j, 1 - mine, 2).start()

    near = [lax.rem(b + k, n) for k in (1, n - 1, 2)]

    def condition(c):
        def step(t, carry):
            cols = pl.ds(pl.multiple_of(t * tile, tile), tile)
            part = jnp.dot(tbuf[c], kbuf[:, cols], preferred_element_type=jnp.float32)
            hi = part.astype(jnp.bfloat16)
            pbuf[c, :rows, cols] = hi
            pbuf[c, rows:, cols] = (part - hi.astype(jnp.float32)).astype(jnp.bfloat16)
            return carry

        lax.fori_loop(0, depth // tile, step, 0)

    def score(c):
        def step(j, carry):
            both_terms = lax.dot_general(
                pbuf[c], rbuf[j], (((1,), (1,)), ((), ())), preferred_element_type=jnp.float32
            )
            sbuf[c, j] = both_terms[:rows] + both_terms[rows:]
            return carry

        lax.fori_loop(0, n, step, 0)
        core_copy(c).start()

    def span(start, size):
        return pl.ds(pl.multiple_of(start, quarter), size)

    own_half = span(core * half, half)
    sib_half = span((1 - core) * half, half)
    own_part = span(core * half + chip * quarter, quarter)
    peer_part = span(core * half + (1 - chip) * quarter, quarter)

    def core_copy(c):
        return remote(sbuf.at[c, :, sib_half], crecv.at[c], csend.at[c], crsem.at[c], b, sib)

    def chip_copy(c):
        return remote(xout.at[c], xrecv.at[c], xsend.at[c], xrsem.at[c], b, peer)

    def plane_copy(c, k):
        to = lax.rem(b + k, n)
        return remote(
            zout.at[c, to], zrecv.at[b, c], zsend.at[c, k - 1], zrsem.at[b, c], to, p
        )

    def join_cores(c):
        core_copy(c).wait_recv()
        sbuf[c, :, own_half] += crecv[c]
        xout[c] = sbuf[c, :, peer_part].astype(xout.dtype)
        chip_copy(c).start()

    def join_chips(c):
        chip_copy(c).wait_recv()
        total = sbuf[c, :, own_part] + xrecv[c].astype(jnp.float32)
        sbuf[c, :, own_part] = total
        zout[c] = total.astype(zout.dtype)
        for k in range(1, n):
            plane_copy(c, k).start()

    def at_step(k, f):
        if k == 0:
            f(b)
        else:
            on(b - k >= 0, f, b - k)
            on(b + k < n, f, b + k)

    on(across, across_arrives)
    arrivals(1)

    @pl.when(entry)
    def _():
        for j in near:
            z_half(j)

    load_t.wait()
    load_k.wait()
    condition(b)
    arrivals(2)

    @pl.when(entry)
    def _():
        for j in near:
            x_half(j)

    at_step(1, condition)
    at_step(2, condition)

    @pl.when(jnp.logical_not(entry))
    def _():
        own_sib.wait_recv()
        for j in near:
            r_move(j, 0, 1).wait_recv()
            r_move(j, 1, 1).wait_recv()

    on(diag, load_r.wait)
    for k in range(n):
        if k > 2:
            arrivals(k)
            at_step(k, condition)
        at_step(k, score)
        at_step(k, join_cores)
        if k > 0:
            at_step(k - 1, join_chips)
    at_step(n - 1, join_chips)

    def home_copy(c):
        return remote(fbuf.at[c], home.at[p], fsend.at[c], frsem.at[p], b, c)

    for c in range(n):
        total = sbuf[c, b, own_part]
        for k in range(1, n):
            j = lax.rem(b + k, n)
            remote(zrecv.at[j, c], zrecv.at[j, c], zsend.at[c, 0], zrsem.at[j, c], j, p).wait_recv()
            total = total + zrecv[j, c].astype(jnp.float32)
        fbuf[c] = total
        on(p != c, home_copy(c).start)
    out_ref[own_part, :] = fbuf[p]
    for q in range(n):
        @pl.when(p != q)
        def _():
            remote(home.at[q], home.at[q], fsend.at[q], frsem.at[q], b, q).wait_recv()
            start = (q % 2) * half + (q // 2) * quarter
            out_ref[start:start + quarter, :] = home[q]

    on(jnp.logical_not(diag), own_top.wait_send)
    on(jnp.logical_not(diag), own_low.wait_send)
    on(diag, own_peer.wait_send)
    on(diag, own_sib.wait_send)
    for part in range(4):
        on(b > 0, t_copy(t_ref, b, 0, part).wait_send)
        on(b < n - 1, t_copy(t_ref, b, 1, part).wait_send)
    on(jnp.logical_not(across), go_on.wait_send)
    on(across, peer_sib.wait_send)

    @pl.when(entry)
    def _():
        for j in near:
            for way in range(2):
                r_move(j, mine, way).wait_send()
            r_move(j, 1 - mine, 2).wait_send()

    for k in range(1, n):
        for part in range(4):
            on(both(b - k >= 0, b < n - 1), t_copy(tbuf.at[b - k], b - k, 1, part).wait_send)
            on(both(b + k < n, b > 0), t_copy(tbuf.at[b + k], b + k, 0, part).wait_send)
    for c in range(n):
        core_copy(c).wait_send()
        chip_copy(c).wait_send()
        for k in range(1, n):
            plane_copy(c, k).wait_send()
        on(p != c, home_copy(c).wait_send)


def fused(n, test_features, train_features, kernel_inverse):
    rows, depth = test_features.shape
    bf16, f32 = jnp.bfloat16, jnp.float32
    dma = pltpu.SemaphoreType.DMA
    return pl.pallas_call(
        functools.partial(kernel, n, min(512, depth)),
        out_shape=jax.ShapeDtypeStruct((rows, rows), f32),
        in_specs=[pl.BlockSpec(memory_space=pl.ANY)] * 3,
        out_specs=pl.BlockSpec(memory_space=pltpu.VMEM),
        scratch_shapes=[
            pltpu.VMEM((n, rows, depth), bf16),
            pltpu.VMEM((n, rows, depth), bf16),
            pltpu.VMEM((rows // 2, depth), bf16),
            pltpu.VMEM((depth, depth), bf16),
            pltpu.VMEM((n, 2 * rows, depth), bf16),
            pltpu.VMEM((n, n, rows, rows), f32),
            pltpu.VMEM((n, n, rows // 2, rows), f32),
            pltpu.VMEM((n, n, rows // 4, rows), bf16),
            pltpu.VMEM((n, n, rows // 4, rows), bf16),
            pltpu.VMEM((n, n, rows // 4, rows), bf16),
            pltpu.VMEM((n, n, rows // 4, rows), bf16),
            pltpu.VMEM((n, rows // 4, rows), f32),
            pltpu.VMEM((n, rows // 4, rows), f32),
            dma((3,)),
            dma((2, n, 4)),
            dma((n, 4)),
            dma((3 + 3 * n,)),
            dma((n, 2)),
            dma,
            dma,
            dma((n,)),
            dma((n,)),
            dma((n,)),
            dma((n,)),
            dma((n, n - 1)),
            dma((n, n)),
            dma((n,)),
            dma((n,)),
        ],
        compiler_params=pltpu.CompilerParams(
            collective_id=0, has_side_effects=True, vmem_limit_bytes=VMEM_BYTES
        ),
        cost_estimate=pl.CostEstimate(
            flops=2 * n * rows * depth * (depth + 2 * n * rows),
            bytes_accessed=2 * depth * (depth + 2 * rows) + 4 * rows * rows,
            transcendentals=0,
        ),
    )(test_features, train_features, kernel_inverse)


def held_bytes(n, rows, depth):
    return 8 * n * rows * depth + 2 * depth * depth + 8 * n * rows * n * rows


def solution(mesh):
    in_specs = (P(("groups", "blk"), "panel"), P(("groups", "blk"), "panel"), P("panel", "blk"))
    out_specs = P(("groups", "panel"), "blk")
    blocks, panels = mesh.shape["blk"], mesh.shape["panel"]

    def run(test_features, train_features, kernel_inverse):
        rows, depth = test_features.shape
        same = train_features.shape == (rows, depth) and kernel_inverse.shape == (depth, depth)
        if blocks == 4 and panels == 4 and same and held_bytes(blocks, rows, depth) < VMEM_BYTES * 3 // 4:
            return fused(blocks, test_features, train_features, kernel_inverse)
        return local(test_features, train_features, kernel_inverse)

    return jax.shard_map(run, mesh=mesh, in_specs=in_specs, out_specs=out_specs, check_vma=False)
```
